32 devices in a mesh: parts: 2 (over y), expert: 4 (over x, core), split: 4 (over z).
Axes of the slice: x: 2, y: 2, z: 4, core: 2. Of those that a mesh axis runs over, the one named last changes fastest.
Arguments:
- tokens: bfloat16 [128, 7168], P(('parts', 'expert', 'split')), parts along dimension 0, may hold values from -6 to 6
- routes: int32 [128, 8], P(('parts', 'expert', 'split')), parts along dimension 0, may hold values from 0 to 15, all different within a row; in each aligned block of 4 rows (0 to 3, 4 to 7, ...) at most 4 rows name the same one
- gates: float32 [128, 8], P(('parts', 'expert', 'split')), parts along dimension 0, may hold values from 0.1 to 1
- w_gate: bfloat16 [16, 7168, 2048], P('expert', None, 'split'), may hold values from -0.0625 to 0.0625
- w_up: bfloat16 [16, 7168, 2048], P('expert', None, 'split'), may hold values from -0.0625 to 0.0625
- w_down: bfloat16 [16, 2048, 7168], P('expert', 'split'), may hold values from -0.125 to 0.125
Outputs:
- mixed: bfloat16 [128, 7168], P(('parts', 'expert', 'split')), parts along dimension 0
The draws below stay inside these ranges and needn't reach their ends.
There are 2 independent parts, one for each index of `parts`. The reference program is written for one: setup_inputs(seed, part) draws one part's arguments, and reference() takes and returns one part's arrays. A program takes and returns all parts, laid end to end along the dimension named above; an argument that names none is the same for every part. Nothing has to cross between parts.
Inputs may be any that keep to these rules, and one draw needn't show every extreme that they name: `routes`: each row names 8 different experts.
All inputs are finite; a program needn't handle non-finite values.
Results may differ from the reference program's by a relative error of at most 0.0058.
Values may be sent and summed in bfloat16 or wider, within the bound.
A program may use at most 320 MiB of HBM per device.

```python
import math
import jax
import jax.numpy as jnp
import numpy as np
from jax import lax

D = 7168
FF = 2048
E = 16
TOP = 8
R = 4
ROWS = 64


def steps_of(rng, dims, pieces, low, top_value):
    def one(dim, parts):
        draws = jax.random.uniform(jax.random.fold_in(jax.random.fold_in(rng, 6), dim), (parts,), jnp.float32, low / len(pieces), top_value / len(pieces))
        return jnp.repeat(jnp.exp(draws), dims[dim] // parts).reshape((-1,) + (1,) * (len(dims) - dim - 1))

    loudness = one(*pieces[0])
    for cut in pieces[1:]:
        loudness = loudness * one(*cut)
    return loudness


def shared_out(key, own, number, rows, amount, top, reach, lean):
    order = jax.random.permutation(key, amount)
    crowded, ordinary = shares(amount, rows * top, reach, lean, True), shares(amount, rows * top, reach, lean, False)
    places = jnp.arange(amount)

    def named(lengths, offset_by):
        used = int((lengths > 0).sum())
        fixed = max(1, used // 4)
        shifted = fixed + (places - fixed + offset_by * (used - fixed)) % max(1, amount - fixed)
        return jnp.zeros((amount,), jnp.int32).at[order[jnp.where(places < fixed, places, shifted)]].set(jnp.asarray(lengths, jnp.int32))

    lengths = jnp.where(number % 4 == 0, named(crowded, number // 4), named(ordinary, number - number // 4 - 1))
    mixed = jax.random.permutation(jax.random.fold_in(own, 3), amount)
    giver, receiver = mixed[0:amount // 2 * 2:2], mixed[1:amount // 2 * 2:2]
    slack = jnp.minimum(lengths[giver] - 1, reach - lengths[receiver]) // 2
    slack = jnp.where((giver == order[0]) | (receiver == order[0]) | (lengths[receiver] == 0), 0, jnp.maximum(slack, 0))
    shifted = jax.random.randint(jax.random.fold_in(own, 4), (amount // 2,), 0, 1 << 20) % (slack + 1)
    lengths = lengths.at[giver].add(-shifted).at[receiver].add(shifted)
    items = jnp.searchsorted(jnp.cumsum(lengths), jnp.arange(rows * top), side="right").astype(jnp.int32)
    listing = items.reshape(top, rows).T
    listing = listing[jax.random.permutation(jax.random.fold_in(own, 1), rows)]
    offset_by = jax.random.randint(jax.random.fold_in(own, 2), (rows, 1), 0, top)
    return jnp.take_along_axis(listing, (jnp.arange(top)[None, :] + offset_by) % top, axis=1)


def shares(count, total, limit, lean, full):
    weights = [(1 << 20) // math.isqrt(rank ** lean) + 1 for rank in range(1, count + 1)]
    largest = limit if full else min(limit, max(-(-total // count), total * weights[0] // sum(weights)))
    least = 1 if total - largest >= count - 1 else 0
    holding, spare = [largest] + [least] * (count - 1), total - largest - least * (count - 1)
    while spare > 0:
        candidates = [i for i in range(1, count) if holding[i] < largest] or [i for i in range(1, count) if holding[i] < limit]
        mass, left = sum([weights[i] for i in candidates]), spare
        for i in candidates:
            extra = min(limit - holding[i], max(1, left * weights[i] // mass), spare)
            holding[i] = holding[i] + extra
            spare = spare - extra
    return np.array(holding)


def scatter_about(rng, dims, deviation, limit, cuts=(), kind=jnp.bfloat16):
    factor_of = steps_of(rng, dims, cuts, -0.22, 0.18) if cuts else 1.0
    values = jax.random.normal(rng, dims, jnp.float32) * deviation * factor_of
    return jnp.minimum(jnp.maximum(values, -limit), limit).astype(kind)


def setup_inputs(seed: int = 0, part: int = 0) -> dict:
    splits = jax.random.split(jax.random.key(seed), 7)
    part_keys = jax.random.split(jax.random.fold_in(splits[6], part), 7)
    tokens = scatter_about(part_keys[0], (ROWS, D), 1.0, 6.0, ((0, 16),))
    routes_keys = jax.random.split(jax.random.fold_in(part_keys[1], 1), ROWS // R)
    routes_turns = jax.random.permutation(jax.random.fold_in(part_keys[1], 3), ROWS // R)
    routes = jax.vmap(lambda own, number: shared_out(jax.random.fold_in(part_keys[1], 2), own, number, R, E, TOP, R, 2))(routes_keys, routes_turns).reshape((ROWS, TOP))
    gates = jnp.clip(0.1 + 0.9 * jax.random.uniform(part_keys[2], (ROWS, TOP), jnp.float32) ** steps_of(part_keys[2], (ROWS, TOP), ((0, 16),), -0.2, 0.2), 0.1, 1.0)
    w_gate = scatter_about(splits[3], (E, D, FF), D ** -0.5, 0.0625, ((0, 4), (2, 4)))
    w_up = scatter_about(splits[4], (E, D, FF), D ** -0.5, 0.0625, ((0, 4), (2, 4)))
    w_down = scatter_about(splits[5], (E, FF, D), FF ** -0.5, 0.125, ((0, 4), (1, 4)))
    return {"tokens": tokens, "routes": routes, "gates": gates, "w_gate": w_gate, "w_up": w_up, "w_down": w_down}


def reference(tokens, routes, gates, w_gate, w_up, w_down):
    def add_expert(total, index):
        gate = jnp.dot(tokens, w_gate[index], preferred_element_type=jnp.float32)
        up = jnp.dot(tokens, w_up[index], preferred_element_type=jnp.float32)
        hidden = (jax.nn.silu(gate) * up).astype(jnp.bfloat16)
        result = jnp.dot(hidden, w_down[index], preferred_element_type=jnp.float32).astype(jnp.bfloat16)
        weight = jnp.sum(jnp.where(routes == index, gates, jnp.float32(0.0)), axis=1)
        return total + weight[:, None] * result.astype(jnp.float32), None

    start = jnp.zeros(tokens.shape, jnp.float32)
    total, unused = lax.scan(add_expert, start, jnp.arange(E, dtype=jnp.int32))
    return total.astype(jnp.bfloat16)
```

```python
import functools

import jax
import jax.numpy as jnp
from jax import lax
from jax.experimental import pallas as pl
from jax.experimental.pallas import tpu as pltpu
from jax.sharding import PartitionSpec as P

MESH = pl.DeviceIdType.MESH
F32, BF16 = jnp.float32, jnp.bfloat16


def selector(rows, columns, factor, offset):
    r = lax.broadcasted_iota(jnp.int32, (rows, columns), 0)
    c = lax.broadcasted_iota(jnp.int32, (rows, columns), 1)
    hit = (c == r * factor + offset) if factor > 0 else (r == c * (-factor) + offset)
    return jnp.where(hit, F32(1), F32(0)).astype(BF16)


def kernel(
    cfg, own_ref, wg_ref, wu_ref, wd_ref, out_ref,
    buf, xs, wts, gu, dn, acc_g, acc_u, hid, part, part2,
    s1, r1, s2, r2, s3, r3,
    gu_sem, dn_sem, agz_sem, agx_sem, agc_sem, ag_recv,
    s1_sem, r1_sem, s2_sem, r2_sem, s3_sem, r3_sem,
):
    NX, NZ, NCORE, R, Q, EL, NG, ND, NC, C, FF = (
        cfg[k] for k in ("NX", "NZ", "NCORE", "R", "Q", "EL", "NG", "ND", "NC", "C", "FF")
    )
    KC = xs.shape[2]
    M = xs.shape[1]
    NGU = EL * Q
    p = lax.axis_index("parts")
    ex = lax.axis_index("expert")
    z = lax.axis_index("split")
    x, core = ex // NCORE, ex % NCORE
    other = (core + 1) % NCORE

    def dev(xx, cc, zz):
        return (p, xx * NCORE + cc, zz)

    def shard(xx, cc, zz):
        return (cc * NX + xx) * NZ + zz

    def gu_copy(i, which):
        e, q = i // Q, i % Q
        src = (wg_ref, wu_ref)[which]
        slot = i % NG
        return pltpu.make_async_copy(
            src.at[e, pl.ds(q * KC, KC), :], gu.at[slot, which], gu_sem.at[slot, which]
        )

    def dn_copy(c):
        slot = c % ND
        return pltpu.make_async_copy(
            wd_ref.at[:, :, pl.ds(pl.multiple_of(c * C, C), C)], dn.at[slot], dn_sem.at[slot]
        )

    for i in range(NG):
        gu_copy(i, 0).start()
        gu_copy(i, 1).start()

    peers = [dev(x, core, (z + k) % NZ) for k in range(1, NZ)]
    peers += [dev((x + k) % NX, core, z) for k in range(1, NX)]
    peers += [dev(x, other, z)]
    barrier = pltpu.get_barrier_semaphore()
    for peer in peers:
        pl.semaphore_signal(barrier, inc=1, device_id=peer, device_id_type=MESH)

    own = shard(x, core, z)
    buf[own] = own_ref[...]
    pl.semaphore_wait(barrier, len(peers))

    def remote(src, dst, send, recv, to):
        return pltpu.make_async_remote_copy(
            src_ref=src, dst_ref=dst, send_sem=send, recv_sem=recv, device_id=to, device_id_type=MESH
        )

    def ag(s, send, to):
        return remote(buf.at[s], buf.at[s], send, ag_recv.at[s], to)

    sends = []

    def go(copy):
        copy.start()
        sends.append(copy)

    def to_x(j):
        s = shard(x, core, (z + j) % NZ)
        for k in range(1, NX):
            go(ag(s, agx_sem.at[j, k - 1], dev((x + k) % NX, core, z)))

    def to_core(i, j):
        s = shard((x + i) % NX, core, (z + j) % NZ)
        go(ag(s, agc_sem.at[i, j], dev(x, other, z)))

    def arrived(s):
        ag(s, agz_sem.at[0], dev(x, other, z)).wait_recv()

    for k in range(1, NZ):
        go(ag(own, agz_sem.at[k - 1], dev(x, core, (z + k) % NZ)))
    to_x(0)
    to_core(0, 0)
    for j in range(1, NZ):
        arrived(shard(x, core, (z + j) % NZ))
        to_x(j)
        to_core(0, j)
    for j in range(NZ):
        for i in range(1, NX):
            arrived(shard((x + i) % NX, core, (z + j) % NZ))
            to_core(i, j)
    for i in range(NX):
        for j in range(NZ):
            arrived(shard((x + i) % NX, other, (z + j) % NZ))

    S = NX * NZ * NCORE
    G = min(S, 16)
    for g in range(S // G):
        rows = pl.ds(g * G * R, G * R)
        block = buf[g * G : (g + 1) * G].reshape(G * R * Q, buf.shape[2])
        weight = None
        for q in range(Q):
            pick = selector(G * R, G * R * Q, Q, q)
            got = jnp.dot(pick, block, preferred_element_type=F32)
            xs[q, rows, :] = got[:, :KC].astype(BF16)
            tail = got[:, KC:]
            weight = tail if weight is None else weight + tail
        wts[rows, :] = weight

    def gu_step(i, carry):
        e, q = i // Q, i % Q
        slot = i % NG
        gu_copy(i, 0).wait()
        gu_copy(i, 1).wait()
        rows = xs[q]
        g = jnp.dot(rows, gu[slot, 0], preferred_element_type=F32)
        u = jnp.dot(rows, gu[slot, 1], preferred_element_type=F32)

        @pl.when(q == 0)
        def _():
            acc_g[...] = g
            acc_u[...] = u

        @pl.when(q > 0)
        def _():
            acc_g[...] += g
            acc_u[...] += u

        @pl.when(q == Q - 1)
        def _():
            lane = lax.broadcasted_iota(jnp.int32, wts.shape, 1)
            scale = jnp.sum(jnp.where(lane == ex * EL + e, wts[...], F32(0)), axis=1, keepdims=True)
            gate = acc_g[...]
            hid[e] = (gate / (1 + jnp.exp(-gate)) * acc_u[...] * scale).astype(BF16)

        nxt = i + NG

        @pl.when(nxt < NGU)
        def _():
            gu_copy(nxt, 0).start()
            gu_copy(nxt, 1).start()

        @pl.when((nxt >= NGU) & (nxt - NGU < ND))
        def _():
            dn_copy(nxt - NGU).start()

        return carry

    lax.fori_loop(0, NGU, gu_step, 0)
    for c in range(NG, ND):
        dn_copy(c).start()

    def send1(c):
        return remote(s1.at[c], r1.at[c], s1_sem.at[c], r1_sem.at[c], dev(x, other, z))

    def send2(c, k):
        return remote(
            s2.at[c, k - 1], r2.at[c, k - 1], s2_sem.at[c, k - 1], r2_sem.at[c, k - 1],
            dev((x + k) % NX, core, z),
        )

    def send3(c, k):
        to = (z + k) % NZ
        return remote(
            s3.at[c, to], r3.at[c, k - 1], s3_sem.at[c, k - 1], r3_sem.at[c, k - 1], dev(x, core, to)
        )

    def down_step(t, carry):
        @pl.when(t < NC)
        def _():
            dn_copy(t).wait()
            slot = t % ND
            total = jnp.dot(hid[0], dn[slot, 0], preferred_element_type=F32)
            for e in range(1, EL):
                total += jnp.dot(hid[e], dn[slot, e], preferred_element_type=F32)
            part[t % 2] = total.reshape(part.shape[1:])
            s1[t] = part[t % 2, other].astype(BF16)
            send1(t).start()

            @pl.when(t + ND < NC)
            def _():
                dn_copy(t + ND).start()

        @pl.when((t >= 1) & (t <= NC))
        def _():
            c = t - 1
            send1(c).wait_recv()
            y = part[c % 2, core] + r1[c].astype(F32)
            part2[c % 2] = y.reshape(part2.shape[1:])
            for k in range(1, NX):
                s2[c, k - 1] = part2[c % 2, (x + k) % NX].astype(BF16)
                send2(c, k).start()

        @pl.when((t >= 2) & (t <= NC + 1))
        def _():
            c = t - 2
            y = part2[c % 2, x]
            for k in range(1, NX):
                send2(c, k).wait_recv()
                y += r2[c, k - 1].astype(F32)
            y = y.astype(BF16)
            w = C // Q
            packed = None
            for q in range(Q):
                pick = selector(NZ * R * Q, NZ * R, -Q, q)
                term = jnp.dot(pick, y[:, q * w : (q + 1) * w], preferred_element_type=F32)
                packed = term if packed is None else packed + term
            s3[c] = packed.astype(BF16).reshape(NZ, R * Q, w)
            for k in range(1, NZ):
                send3(c, k).start()

        @pl.when(t >= 3)
        def _():
            c = t - 3
            y = s3[c, z].astype(F32)
            for k in range(1, NZ):
                send3(c, k).wait_recv()
                y += r3[c, k - 1].astype(F32)
            out_ref[c] = y.astype(BF16)

        return carry

    lax.fori_loop(0, NC + 3, down_step, 0)

    for copy in sends:
        copy.wait_send()

    def finish(c, carry):
        send1(c).wait_send()
        for k in range(1, NX):
            send2(c, k).wait_send()
        for k in range(1, NZ):
            send3(c, k).wait_send()
        return carry

    lax.fori_loop(0, NC, finish, 0)


def shards(tokens, routes, gates, w_gate, w_up, w_down):
    n_expert, n_split = lax.axis_size("expert"), lax.axis_size("split")
    R, D = tokens.shape
    EL, _, FF = w_gate.shape
    experts = n_expert * EL
    Q = 16 // R
    NCORE = 2
    NX, NZ = n_expert // NCORE, n_split
    KC = D // Q
    C = 1024
    NC = D // C
    NG, ND = min(7, EL * Q), min(5, NC)
    M = NX * NZ * NCORE * R
    S = NX * NZ * NCORE
    cfg = dict(NX=NX, NZ=NZ, NCORE=NCORE, R=R, Q=Q, EL=EL, NG=NG, ND=ND, NC=NC, C=C, FF=FF)

    named = routes[:, :, None] == jnp.arange(experts, dtype=jnp.int32)
    weight = jnp.sum(jnp.where(named, gates[:, :, None], F32(0)), axis=1)
    hi = lax.reduce_precision(weight, 8, 7)
    mid = lax.reduce_precision(weight - hi, 8, 7)
    low = weight - hi - mid
    terms = jnp.stack([hi, mid, low] + [jnp.zeros_like(hi)] * (Q - 3), axis=1).astype(BF16)
    terms = jnp.pad(terms, ((0, 0), (0, 0), (0, 128 - experts)))
    own = jnp.concatenate([tokens.reshape(R, Q, KC), terms], axis=2).reshape(R * Q, KC + 128)

    any_space = pl.BlockSpec(memory_space=pl.ANY)
    vmem = pl.BlockSpec(memory_space=pltpu.VMEM)
    dma = pltpu.SemaphoreType.DMA
    out = pl.pallas_call(
        functools.partial(kernel, cfg),
        out_shape=jax.ShapeDtypeStruct((NC, R * Q, C // Q), BF16),
        in_specs=[vmem, any_space, any_space, any_space],
        out_specs=vmem,
        scratch_shapes=[
            pltpu.VMEM((S, R * Q, KC + 128), BF16),
            pltpu.VMEM((Q, M, KC), BF16),
            pltpu.VMEM((M, 128), F32),
            pltpu.VMEM((NG, 2, KC, FF), BF16),
            pltpu.VMEM((ND, EL, FF, C), BF16),
            pltpu.VMEM((M, FF), F32),
            pltpu.VMEM((M, FF), F32),
            pltpu.VMEM((EL, M, FF), BF16),
            pltpu.VMEM((2, NCORE, M // NCORE, C), F32),
            pltpu.VMEM((2, NX, NZ * R, C), F32),
            pltpu.VMEM((NC, M // NCORE, C), BF16),
            pltpu.VMEM((NC, M // NCORE, C), BF16),
            pltpu.VMEM((NC, NX - 1, NZ * R, C), BF16),
            pltpu.VMEM((NC, NX - 1, NZ * R, C), BF16),
            pltpu.VMEM((NC, NZ, R * Q, C // Q), BF16),
            pltpu.VMEM((NC, NZ - 1, R * Q, C // Q), BF16),
            dma((NG, 2)), dma((ND,)), dma((NZ - 1,)), dma((NZ, NX - 1)), dma((NX, NZ)), dma((S,)),
            dma((NC,)), dma((NC,)), dma((NC, NX - 1)), dma((NC, NX - 1)), dma((NC, NZ - 1)), dma((NC, NZ - 1)),
        ],
        compiler_params=pltpu.CompilerParams(
            collective_id=0, has_side_effects=True, vmem_limit_bytes=60 * 1024 * 1024
        ),
        cost_estimate=pl.CostEstimate(
            flops=6 * M * EL * D * FF, bytes_accessed=6 * EL * D * FF, transcendentals=M * EL * FF
        ),
        name="expert_layer",
    )(own, w_gate, w_up, w_down)
    return out.reshape(NC, R, Q, C // Q).transpose(1, 0, 2, 3).reshape(R, D)


def solution(mesh):
    in_specs = (
        P(("parts", "expert", "split"), None),
        P(("parts", "expert", "split"), None),
        P(("parts", "expert", "split"), None),
        P("expert", None, "split"),
        P("expert", None, "split"),
        P("expert", "split", None),
    )
    out_specs = P(("parts", "expert", "split"), None)
    return jax.shard_map(shards, mesh=mesh, in_specs=in_specs, out_specs=out_specs, check_vma=False)
```

```python
import functools

import jax
import jax.numpy as jnp
from jax import lax
from jax.experimental import pallas as pl
from jax.experimental.pallas import tpu as pltpu
from jax.sharding import PartitionSpec as P

MESH = pl.DeviceIdType.MESH
F32, BF16 = jnp.float32, jnp.bfloat16
LAG = 2


def selector(rows, columns, factor, offset):
    r = lax.broadcasted_iota(jnp.int32, (rows, columns), 0)
    c = lax.broadcasted_iota(jnp.int32, (rows, columns), 1)
    hit = (c == r * factor + offset) if factor > 0 else (r == c * (-factor) + offset)
    return jnp.where(hit, F32(1), F32(0)).astype(BF16)


def kernel(
    cfg, tok_ref, routes_ref, gates_ref, wg_ref, wu_ref, wd_ref, out_ref,
    buf, xs, wts, gu, dn, acc_g, acc_u, hid, part, part2,
    s1, r1, s2, r2, s3, r3,
    gu_sem, dn_sem, agz_sem, agx_sem, agc_sem, ag_recv,
    s1_sem, r1_sem, s2_sem, r2_sem, s3_sem, r3_sem,
):
    NX, NZ, NCORE, R, Q, EL, NG, ND, NC, C, FF = (
        cfg[k] for k in ("NX", "NZ", "NCORE", "R", "Q", "EL", "NG", "ND", "NC", "C", "FF")
    )
    KC = xs.shape[2]
    M = xs.shape[1]
    NGU = EL * Q
    p = lax.axis_index("parts")
    ex = lax.axis_index("expert")
    z = lax.axis_index("split")
    x, core = ex // NCORE, ex % NCORE
    other = (core + 1) % NCORE

    def dev(xx, cc, zz):
        return (p, xx * NCORE + cc, zz)

    def shard(xx, cc, zz):
        return (cc * NX + xx) * NZ + zz

    def gu_copy(i, which):
        e, q = i // Q, i % Q
        src = (wg_ref, wu_ref)[which]
        slot = i % NG
        return pltpu.make_async_copy(
            src.at[e, pl.ds(q * KC, KC), :], gu.at[slot, which], gu_sem.at[slot, which]
        )

    def dn_copy(c):
        slot = c % ND
        return pltpu.make_async_copy(
            wd_ref.at[:, :, pl.ds(pl.multiple_of(c * C, C), C)], dn.at[slot], dn_sem.at[slot]
        )

    for i in range(NG):
        gu_copy(i, 0).start()
        gu_copy(i, 1).start()

    peers = [dev(x, core, (z + k) % NZ) for k in range(1, NZ)]
    peers += [dev((x + k) % NX, core, z) for k in range(1, NX)]
    peers += [dev(x, other, z)]
    barrier = pltpu.get_barrier_semaphore()
    for peer in peers:
        pl.semaphore_signal(barrier, inc=1, device_id=peer, device_id_type=MESH)

    own = shard(x, core, z)
    routes, gates = routes_ref[...], gates_ref[...]
    lane = lax.broadcasted_iota(jnp.int32, (R, 128), 1)
    rest = jnp.zeros((R, 128), F32)
    for k in range(routes.shape[1]):
        rest += jnp.where(routes[:, k : k + 1] == lane, gates[:, k : k + 1], F32(0))
    mine, tail = None, None
    for q in range(Q):
        place = selector(R * Q, R, -Q, q)
        term = jnp.dot(place, tok_ref[:, q * KC : (q + 1) * KC], preferred_element_type=F32)
        mine = term if mine is None else mine + term
        if q < 3:
            piece = rest.astype(BF16)
            rest = rest - piece.astype(F32)
            term = jnp.dot(place, piece, preferred_element_type=F32)
            tail = term if tail is None else tail + term
    buf[own, :, :KC] = mine.astype(BF16)
    buf[own, :, KC:] = tail.astype(BF16)
    pl.semaphore_wait(barrier, len(peers))

    def remote(src, dst, send, recv, to):
        return pltpu.make_async_remote_copy(
            src_ref=src, dst_ref=dst, send_sem=send, recv_sem=recv, device_id=to, device_id_type=MESH
        )

    def ag(s, send, to):
        return remote(buf.at[s], buf.at[s], send, ag_recv.at[s], to)

    sends = []

    def go(copy):
        copy.start()
        sends.append(copy)

    def to_x(j):
        s = shard(x, core, (z + j) % NZ)
        for k in range(1, NX):
            go(ag(s, agx_sem.at[j, k - 1], dev((x + k) % NX, core, z)))

    def to_core(i, j):
        s = shard((x + i) % NX, core, (z + j) % NZ)
        go(ag(s, agc_sem.at[i, j], dev(x, other, z)))

    def arrived(s):
        ag(s, agz_sem.at[0], dev(x, other, z)).wait_recv()

    for k in range(1, NZ):
        go(ag(own, agz_sem.at[k - 1], dev(x, core, (z + k) % NZ)))
    to_x(0)
    to_core(0, 0)
    for j in range(1, NZ):
        arrived(shard(x, core, (z + j) % NZ))
        to_x(j)
        to_core(0, j)
    for j in range(NZ):
        for i in range(1, NX):
            arrived(shard((x + i) % NX, core, (z + j) % NZ))
            to_core(i, j)
    for i in range(NX):
        for j in range(NZ):
            arrived(shard((x + i) % NX, other, (z + j) % NZ))

    S = NX * NZ * NCORE
    G = min(S, 16)
    for g in range(S // G):
        rows = pl.ds(g * G * R, G * R)
        block = buf[g * G : (g + 1) * G].reshape(G * R * Q, buf.shape[2])
        weight = None
        for q in range(Q):
            pick = selector(G * R, G * R * Q, Q, q)
            got = jnp.dot(pick, block, preferred_element_type=F32)
            xs[q, rows, :] = got[:, :KC].astype(BF16)
            tail = got[:, KC:]
            weight = tail if weight is None else weight + tail
        wts[rows, :] = weight

    def gu_step(i, carry):
        e, q = i // Q, i % Q
        slot = i % NG
        gu_copy(i, 0).wait()
        gu_copy(i, 1).wait()
        rows = xs[q]
        g = jnp.dot(rows, gu[slot, 0], preferred_element_type=F32)
        u = jnp.dot(rows, gu[slot, 1], preferred_element_type=F32)

        @pl.when(q == 0)
        def _():
            acc_g[...] = g
            acc_u[...] = u

        @pl.when(q > 0)
        def _():
            acc_g[...] += g
            acc_u[...] += u

        @pl.when(q == Q - 1)
        def _():
            lane = lax.broadcasted_iota(jnp.int32, wts.shape, 1)
            scale = jnp.sum(jnp.where(lane == ex * EL + e, wts[...], F32(0)), axis=1, keepdims=True)
            gate = acc_g[...]
            hid[e] = (gate / (1 + jnp.exp(-gate)) * acc_u[...] * scale).astype(BF16)

        nxt = i + NG

        @pl.when(nxt < NGU)
        def _():
            gu_copy(nxt, 0).start()
            gu_copy(nxt, 1).start()

        @pl.when((nxt >= NGU) & (nxt - NGU < ND))
        def _():
            dn_copy(nxt - NGU).start()

        return carry

    lax.fori_loop(0, NGU, gu_step, 0)
    for c in range(NG, ND):
        dn_copy(c).start()

    def send1(c):
        return remote(s1.at[c], r1.at[c], s1_sem.at[c], r1_sem.at[c], dev(x, other, z))

    def send2(c, k):
        return remote(
            s2.at[c, k - 1], r2.at[c, k - 1], s2_sem.at[c, k - 1], r2_sem.at[c, k - 1],
            dev((x + k) % NX, core, z),
        )

    def send3(c, k):
        to = (z + k) % NZ
        return remote(
            s3.at[c, to], r3.at[c, k - 1], s3_sem.at[c, k - 1], r3_sem.at[c, k - 1], dev(x, core, to)
        )

    def down_step(t, carry):
        @pl.when(t < NC)
        def _():
            dn_copy(t).wait()
            slot = t % ND
            total = jnp.dot(hid[0], dn[slot, 0], preferred_element_type=F32)
            for e in range(1, EL):
                total += jnp.dot(hid[e], dn[slot, e], preferred_element_type=F32)
            part[t % (LAG + 1)] = total.reshape(part.shape[1:])
            s1[t] = part[t % (LAG + 1), other].astype(BF16)
            send1(t).start()

            @pl.when(t + ND < NC)
            def _():
                dn_copy(t + ND).start()

        @pl.when((t >= LAG) & (t < NC + LAG))
        def _():
            c = t - LAG
            send1(c).wait_recv()
            y = part[c % (LAG + 1), core] + r1[c].astype(F32)
            part2[c % (LAG + 1)] = y.reshape(part2.shape[1:])
            for k in range(1, NX):
                s2[c, k - 1] = part2[c % (LAG + 1), (x + k) % NX].astype(BF16)
                send2(c, k).start()

        @pl.when((t >= 2 * LAG) & (t < NC + 2 * LAG))
        def _():
            c = t - 2 * LAG
            y = part2[c % (LAG + 1), x]
            for k in range(1, NX):
                send2(c, k).wait_recv()
                y += r2[c, k - 1].astype(F32)
            y = y.astype(BF16)
            w = C // Q
            packed = None
            for q in range(Q):
                pick = selector(NZ * R * Q, NZ * R, -Q, q)
                term = jnp.dot(pick, y[:, q * w : (q + 1) * w], preferred_element_type=F32)
                packed = term if packed is None else packed + term
            s3[c] = packed.astype(BF16).reshape(NZ, R * Q, w)
            for k in range(1, NZ):
                send3(c, k).start()

        @pl.when(t >= 3 * LAG)
        def _():
            c = t - 3 * LAG
            y = s3[c, z].astype(F32)
            for k in range(1, NZ):
                send3(c, k).wait_recv()
                y += r3[c, k - 1].astype(F32)
            y = y.astype(BF16)
            w = C // Q
            for q in range(Q):
                pick = selector(R, R * Q, Q, q)
                piece = jnp.dot(pick, y, preferred_element_type=F32).astype(BF16)
                out_ref[:, pl.ds(pl.multiple_of(c * C + q * w, 128), w)] = piece

        return carry

    lax.fori_loop(0, NC + 3 * LAG, down_step, 0)

    for copy in sends:
        copy.wait_send()

    def finish(c, carry):
        send1(c).wait_send()
        for k in range(1, NX):
            send2(c, k).wait_send()
        for k in range(1, NZ):
            send3(c, k).wait_send()
        return carry

    lax.fori_loop(0, NC, finish, 0)


def shards(tokens, routes, gates, w_gate, w_up, w_down):
    n_expert, n_split = lax.axis_size("expert"), lax.axis_size("split")
    R, D = tokens.shape
    EL, _, FF = w_gate.shape
    Q = 16 // R
    NCORE = 2
    NX, NZ = n_expert // NCORE, n_split
    KC = D // Q
    C = 1024
    NC = D // C
    NG, ND = min(7, EL * Q), min(5, NC)
    M = NX * NZ * NCORE * R
    S = NX * NZ * NCORE
    cfg = dict(NX=NX, NZ=NZ, NCORE=NCORE, R=R, Q=Q, EL=EL, NG=NG, ND=ND, NC=NC, C=C, FF=FF)

    any_space = pl.BlockSpec(memory_space=pl.ANY)
    vmem = pl.BlockSpec(memory_space=pltpu.VMEM)
    dma = pltpu.SemaphoreType.DMA
    out = pl.pallas_call(
        functools.partial(kernel, cfg),
        out_shape=jax.ShapeDtypeStruct((R, D), BF16),
        in_specs=[vmem, vmem, vmem, any_space, any_space, any_space],
        out_specs=vmem,
        scratch_shapes=[
            pltpu.VMEM((S, R * Q, KC + 128), BF16),
            pltpu.VMEM((Q, M, KC), BF16),
            pltpu.VMEM((M, 128), F32),
            pltpu.VMEM((NG, 2, KC, FF), BF16),
            pltpu.VMEM((ND, EL, FF, C), BF16),
            pltpu.VMEM((M, FF), F32),
            pltpu.VMEM((M, FF), F32),
            pltpu.VMEM((EL, M, FF), BF16),
            pltpu.VMEM((LAG + 1, NCORE, M // NCORE, C), F32),
            pltpu.VMEM((LAG + 1, NX, NZ * R, C), F32),
            pltpu.VMEM((NC, M // NCORE, C), BF16),
            pltpu.VMEM((NC, M // NCORE, C), BF16),
            pltpu.VMEM((NC, NX - 1, NZ * R, C), BF16),
            pltpu.VMEM((NC, NX - 1, NZ * R, C), BF16),
            pltpu.VMEM((NC, NZ, R * Q, C // Q), BF16),
            pltpu.VMEM((NC, NZ - 1, R * Q, C // Q), BF16),
            dma((NG, 2)), dma((ND,)), dma((NZ - 1,)), dma((NZ, NX - 1)), dma((NX, NZ)), dma((S,)),
            dma((NC,)), dma((NC,)), dma((NC, NX - 1)), dma((NC, NX - 1)), dma((NC, NZ - 1)), dma((NC, NZ - 1)),
        ],
        compiler_params=pltpu.CompilerParams(
            collective_id=0, has_side_effects=True, vmem_limit_bytes=60 * 1024 * 1024
        ),
        cost_estimate=pl.CostEstimate(
            flops=6 * M * EL * D * FF, bytes_accessed=6 * EL * D * FF, transcendentals=M * EL * FF
        ),
        name="expert_layer",
    )(tokens, routes, gates, w_gate, w_up, w_down)
    return out


def solution(mesh):
    in_specs = (
        P(("parts", "expert", "split"), None),
        P(("parts", "expert", "split"), None),
        P(("parts", "expert", "split"), None),
        P("expert", None, "split"),
        P("expert", None, "split"),
        P("expert", "split", None),
    )
    out_specs = P(("parts", "expert", "split"), None)
    return jax.shard_map(shards, mesh=mesh, in_specs=in_specs, out_specs=out_specs, check_vma=False)
```

```python
import functools

import jax
import jax.numpy as jnp
from jax import lax
from jax.experimental import pallas as pl
from jax.experimental.pallas import tpu as pltpu
from jax.sharding import PartitionSpec as P

MESH = pl.DeviceIdType.MESH
F32, BF16 = jnp.float32, jnp.bfloat16
LAG = 2


def selector(rows, columns, factor, offset):
    r = lax.broadcasted_iota(jnp.int32, (rows, columns), 0)
    c = lax.broadcasted_iota(jnp.int32, (rows, columns), 1)
    hit = (c == r * factor + offset) if factor > 0 else (r == c * (-factor) + offset)
    return jnp.where(hit, F32(1), F32(0)).astype(BF16)


def kernel(
    cfg, tok_ref, routes_ref, gates_ref, wg_ref, wu_ref, wd_ref, out_ref,
    buf, xs, wts, gu, dn, acc_g, acc_u, hid, part, part2,
    s1, r1, s2, r2, s3, r3,
    gu_sem, dn_sem, agz_sem, agx_sem, agc_sem, ag_recv,
    s1_sem, r1_sem, s2_sem, r2_sem, s3_sem, r3_sem,
):
    NX, NZ, NCORE, R, Q, EL, NG, ND, NC, C, FF = (
        cfg[k] for k in ("NX", "NZ", "NCORE", "R", "Q", "EL", "NG", "ND", "NC", "C", "FF")
    )
    KC = xs.shape[2]
    M = xs.shape[1]
    NGU = EL * Q
    p = lax.axis_index("parts")
    ex = lax.axis_index("expert")
    z = lax.axis_index("split")
    x, core = ex // NCORE, ex % NCORE
    other = (core + 1) % NCORE

    def dev(xx, cc, zz):
        return (p, xx * NCORE + cc, zz)

    def shard(xx, cc, zz):
        return (cc * NX + xx) * NZ + zz

    def gu_copy(i, which):
        e, q = i // Q, i % Q
        src = (wg_ref, wu_ref)[which]
        slot = i % NG
        return pltpu.make_async_copy(
            src.at[e, pl.ds(q * KC, KC), :], gu.at[slot, which], gu_sem.at[slot, which]
        )

    def dn_copy(c):
        slot = c % ND
        return pltpu.make_async_copy(
            wd_ref.at[:, :, pl.ds(pl.multiple_of(c * C, C), C)], dn.at[slot], dn_sem.at[slot]
        )

    for i in range(NG):
        gu_copy(i, 0).start()
        gu_copy(i, 1).start()
    for c in range(ND):
        dn_copy(c).start()

    peers = [dev(x, core, (z + k) % NZ) for k in range(1, NZ)]
    peers += [dev((x + k) % NX, core, z) for k in range(1, NX)]
    peers += [dev(x, other, z)]
    barrier = pltpu.get_barrier_semaphore()
    for peer in peers:
        pl.semaphore_signal(barrier, inc=1, device_id=peer, device_id_type=MESH)

    own = shard(x, core, z)
    routes, gates = routes_ref[...], gates_ref[...]
    lane = lax.broadcasted_iota(jnp.int32, (R, 128), 1)
    rest = jnp.zeros((R, 128), F32)
    for k in range(routes.shape[1]):
        rest += jnp.where(routes[:, k : k + 1] == lane, gates[:, k : k + 1], F32(0))
    mine, tail = None, None
    for q in range(Q):
        place = selector(R * Q, R, -Q, q)
        term = jnp.dot(place, tok_ref[:, q * KC : (q + 1) * KC], preferred_element_type=F32)
        mine = term if mine is None else mine + term
        if q < 3:
            piece = rest.astype(BF16)
            rest = rest - piece.astype(F32)
            term = jnp.dot(place, piece, preferred_element_type=F32)
            tail = term if tail is None else tail + term
    buf[own, :, :KC] = mine.astype(BF16)
    buf[own, :, KC:] = tail.astype(BF16)
    pl.semaphore_wait(barrier, len(peers))

    def remote(src, dst, send, recv, to):
        return pltpu.make_async_remote_copy(
            src_ref=src, dst_ref=dst, send_sem=send, recv_sem=recv, device_id=to, device_id_type=MESH
        )

    def ag(s, send, to):
        return remote(buf.at[s], buf.at[s], send, ag_recv.at[s], to)

    sends = []

    def go(copy):
        copy.start()
        sends.append(copy)

    def peer_z(j):
        if NZ != 4:
            return (z + j) % NZ
        return (z, z + 1 - 2 * (z % 2), (z + 2) % 4, 3 - z)[j]

    def to_x(j):
        s = shard(x, core, peer_z(j))
        for k in range(1, NX):
            go(ag(s, agx_sem.at[j, k - 1], dev((x + k) % NX, core, z)))

    def to_core(i, j):
        s = shard((x + i) % NX, core, peer_z(j))
        go(ag(s, agc_sem.at[i, j], dev(x, other, z)))

    def arrived(s):
        ag(s, agz_sem.at[0], dev(x, other, z)).wait_recv()

    for k in range(1, NZ):
        go(ag(own, agz_sem.at[k - 1], dev(x, core, peer_z(k))))
    to_x(0)
    to_core(0, 0)
    for j in range(1, NZ):
        arrived(shard(x, core, peer_z(j)))
        to_x(j)
        to_core(0, j)
    for j in range(NZ):
        for i in range(1, NX):
            arrived(shard((x + i) % NX, core, peer_z(j)))
            to_core(i, j)
    for i in range(NX):
        for j in range(NZ):
            arrived(shard((x + i) % NX, other, (z + j) % NZ))

    S = NX * NZ * NCORE
    G = min(S, 16)
    for g in range(S // G):
        rows = pl.ds(g * G * R, G * R)
        block = buf[g * G : (g + 1) * G].reshape(G * R * Q, buf.shape[2])
        weight = None
        for q in range(Q):
            pick = selector(G * R, G * R * Q, Q, q)
            got = jnp.dot(pick, block, preferred_element_type=F32)
            xs[q, rows, :] = got[:, :KC].astype(BF16)
            tail = got[:, KC:]
            weight = tail if weight is None else weight + tail
        wts[rows, :] = weight

    def gu_step(i, carry):
        e, q = i // Q, i % Q
        slot = i % NG
        gu_copy(i, 0).wait()
        gu_copy(i, 1).wait()
        rows = xs[q]
        g = jnp.dot(rows, gu[slot, 0], preferred_element_type=F32)
        u = jnp.dot(rows, gu[slot, 1], preferred_element_type=F32)

        @pl.when(q == 0)
        def _():
            acc_g[...] = g
            acc_u[...] = u

        @pl.when(q > 0)
        def _():
            acc_g[...] += g
            acc_u[...] += u

        @pl.when(q == Q - 1)
        def _():
            lane = lax.broadcasted_iota(jnp.int32, wts.shape, 1)
            scale = jnp.sum(jnp.where(lane == ex * EL + e, wts[...], F32(0)), axis=1, keepdims=True)
            gate = acc_g[...]
            hid[e] = (gate / (1 + jnp.exp(-gate)) * acc_u[...] * scale).astype(BF16)

        nxt = i + NG

        @pl.when(nxt < NGU)
        def _():
            gu_copy(nxt, 0).start()
            gu_copy(nxt, 1).start()

        return carry

    lax.fori_loop(0, NGU, gu_step, 0)

    def send1(c):
        return remote(s1.at[c], r1.at[c], s1_sem.at[c], r1_sem.at[c], dev(x, other, z))

    def send2(c, k):
        return remote(
            s2.at[c, k - 1], r2.at[c, k - 1], s2_sem.at[c, k - 1], r2_sem.at[c, k - 1],
            dev((x + k) % NX, core, z),
        )

    def send3(c, k):
        to = (z + k) % NZ
        return remote(
            s3.at[c, to], r3.at[c, k - 1], s3_sem.at[c, k - 1], r3_sem.at[c, k - 1], dev(x, core, to)
        )

    def down_step(t, carry):
        @pl.when(t < NC)
        def _():
            dn_copy(t).wait()
            slot = t % ND
            total = jnp.dot(hid[0], dn[slot, 0], preferred_element_type=F32)
            for e in range(1, EL):
                total += jnp.dot(hid[e], dn[slot, e], preferred_element_type=F32)
            part[t % (LAG + 1)] = total.reshape(part.shape[1:])
            s1[t] = part[t % (LAG + 1), other].astype(BF16)
            send1(t).start()

            @pl.when(t + ND < NC)
            def _():
                dn_copy(t + ND).start()

        @pl.when((t >= LAG) & (t < NC + LAG))
        def _():
            c = t - LAG
            send1(c).wait_recv()
            y = part[c % (LAG + 1), core] + r1[c].astype(F32)
            part2[c % (LAG + 1)] = y.reshape(part2.shape[1:])
            for k in range(1, NX):
                s2[c, k - 1] = part2[c % (LAG + 1), (x + k) % NX].astype(BF16)
                send2(c, k).start()

        @pl.when((t >= 2 * LAG) & (t < NC + 2 * LAG))
        def _():
            c = t - 2 * LAG
            y = part2[c % (LAG + 1), x]
            for k in range(1, NX):
                send2(c, k).wait_recv()
                y += r2[c, k - 1].astype(F32)
            y = y.astype(BF16)
            w = C // Q
            packed = None
            for q in range(Q):
                pick = selector(NZ * R * Q, NZ * R, -Q, q)
                term = jnp.dot(pick, y[:, q * w : (q + 1) * w], preferred_element_type=F32)
                packed = term if packed is None else packed + term
            s3[c] = packed.astype(BF16).reshape(NZ, R * Q, w)
            for k in range(1, NZ):
                send3(c, k).start()

        @pl.when(t >= 3 * LAG)
        def _():
            c = t - 3 * LAG
            y = s3[c, z].astype(F32)
            for k in range(1, NZ):
                send3(c, k).wait_recv()
                y += r3[c, k - 1].astype(F32)
            y = y.astype(BF16)
            w = C // Q
            for q in range(Q):
                pick = selector(R, R * Q, Q, q)
                piece = jnp.dot(pick, y, preferred_element_type=F32).astype(BF16)
                out_ref[:, pl.ds(pl.multiple_of(c * C + q * w, 128), w)] = piece

        return carry

    lax.fori_loop(0, NC + 3 * LAG, down_step, 0)

    for copy in sends:
        copy.wait_send()

    def finish(c, carry):
        send1(c).wait_send()
        for k in range(1, NX):
            send2(c, k).wait_send()
        for k in range(1, NZ):
            send3(c, k).wait_send()
        return carry

    lax.fori_loop(0, NC, finish, 0)


def shards(tokens, routes, gates, w_gate, w_up, w_down):
    n_expert, n_split = lax.axis_size("expert"), lax.axis_size("split")
    R, D = tokens.shape
    EL, _, FF = w_gate.shape
    Q = 16 // R
    NCORE = 2
    NX, NZ = n_expert // NCORE, n_split
    KC = D // Q
    C = 1024
    NC = D // C
    NG, ND = min(7, EL * Q), min(5, NC)
    M = NX * NZ * NCORE * R
    S = NX * NZ * NCORE
    cfg = dict(NX=NX, NZ=NZ, NCORE=NCORE, R=R, Q=Q, EL=EL, NG=NG, ND=ND, NC=NC, C=C, FF=FF)

    any_space = pl.BlockSpec(memory_space=pl.ANY)
    vmem = pl.BlockSpec(memory_space=pltpu.VMEM)
    dma = pltpu.SemaphoreType.DMA
    out = pl.pallas_call(
        functools.partial(kernel, cfg),
        out_shape=jax.ShapeDtypeStruct((R, D), BF16),
        in_specs=[vmem, vmem, vmem, any_space, any_space, any_space],
        out_specs=vmem,
        scratch_shapes=[
            pltpu.VMEM((S, R * Q, KC + 128), BF16),
            pltpu.VMEM((Q, M, KC), BF16),
            pltpu.VMEM((M, 128), F32),
            pltpu.VMEM((NG, 2, KC, FF), BF16),
            pltpu.VMEM((ND, EL, FF, C), BF16),
            pltpu.VMEM((M, FF), F32),
            pltpu.VMEM((M, FF), F32),
            pltpu.VMEM((EL, M, FF), BF16),
            pltpu.VMEM((LAG + 1, NCORE, M // NCORE, C), F32),
            pltpu.VMEM((LAG + 1, NX, NZ * R, C), F32),
            pltpu.VMEM((NC, M // NCORE, C), BF16),
            pltpu.VMEM((NC, M // NCORE, C), BF16),
            pltpu.VMEM((NC, NX - 1, NZ * R, C), BF16),
            pltpu.VMEM((NC, NX - 1, NZ * R, C), BF16),
            pltpu.VMEM((NC, NZ, R * Q, C // Q), BF16),
            pltpu.VMEM((NC, NZ - 1, R * Q, C // Q), BF16),
            dma((NG, 2)), dma((ND,)), dma((NZ - 1,)), dma((NZ, NX - 1)), dma((NX, NZ)), dma((S,)),
            dma((NC,)), dma((NC,)), dma((NC, NX - 1)), dma((NC, NX - 1)), dma((NC, NZ - 1)), dma((NC, NZ - 1)),
        ],
        compiler_params=pltpu.CompilerParams(
            collective_id=0, has_side_effects=True, vmem_limit_bytes=60 * 1024 * 1024
        ),
        cost_estimate=pl.CostEstimate(
            flops=6 * M * EL * D * FF, bytes_accessed=6 * EL * D * FF, transcendentals=M * EL * FF
        ),
        name="expert_layer",
    )(tokens, routes, gates, w_gate, w_up, w_down)
    return out


def solution(mesh):
    in_specs = (
        P(("parts", "expert", "split"), None),
        P(("parts", "expert", "split"), None),
        P(("parts", "expert", "split"), None),
        P("expert", None, "split"),
        P("expert", None, "split"),
        P("expert", "split", None),
    )
    out_specs = P(("parts", "expert", "split"), None)
    return jax.shard_map(shards, mesh=mesh, in_specs=in_specs, out_specs=out_specs, check_vma=False)
```

```python
import functools

import jax
import jax.numpy as jnp
from jax import lax
from jax.experimental import pallas as pl
from jax.experimental.pallas import tpu as pltpu
from jax.sharding import PartitionSpec as P

MESH = pl.DeviceIdType.MESH
F32, BF16 = jnp.float32, jnp.bfloat16
LAG = 4


def selector(rows, columns, factor, offset):
    r = lax.broadcasted_iota(jnp.int32, (rows, columns), 0)
    c = lax.broadcasted_iota(jnp.int32, (rows, columns), 1)
    hit = (c == r * factor + offset) if factor > 0 else (r == c * (-factor) + offset)
    return jnp.where(hit, F32(1), F32(0)).astype(BF16)


def kernel(
    cfg, tok_ref, routes_ref, gates_ref, wg_ref, wu_ref, wd_ref, out_ref,
    buf, xs, wts, gu, dn, acc_g, acc_u, hid, part, part2,
    s1, r1, s2, r2, s3, r3,
    gu_sem, dn_sem, agz_sem, agx_sem, agc_sem, ag_recv,
    s1_sem, r1_sem, s2_sem, r2_sem, s3_sem, r3_sem,
):
    NX, NZ, NCORE, R, Q, EL, NG, ND, NC, C, FF = (
        cfg[k] for k in ("NX", "NZ", "NCORE", "R", "Q", "EL", "NG", "ND", "NC", "C", "FF")
    )
    KC = xs.shape[2]
    M = xs.shape[1]
    NGU = EL * Q
    p = lax.axis_index("parts")
    ex = lax.axis_index("expert")
    z = lax.axis_index("split")
    x, core = ex // NCORE, ex % NCORE
    other = (core + 1) % NCORE

    def dev(xx, cc, zz):
        return (p, xx * NCORE + cc, zz)

    def shard(xx, cc, zz):
        return (cc * NX + xx) * NZ + zz

    def gu_copy(i, which):
        e, q = i // Q, i % Q
        src = (wg_ref, wu_ref)[which]
        slot = i % NG
        return pltpu.make_async_copy(
            src.at[e, pl.ds(q * KC, KC), :], gu.at[slot, which], gu_sem.at[slot, which]
        )

    def dn_copy(c):
        slot = c % ND
        return pltpu.make_async_copy(
            wd_ref.at[:, :, pl.ds(pl.multiple_of(c * C, C), C)], dn.at[slot], dn_sem.at[slot]
        )

    for i in range(NG):
        gu_copy(i, 0).start()
        gu_copy(i, 1).start()
    for c in range(ND):
        dn_copy(c).start()

    peers = [dev(x, core, (z + k) % NZ) for k in range(1, NZ)]
    peers += [dev((x + k) % NX, core, z) for k in range(1, NX)]
    peers += [dev(x, other, z)]
    barrier = pltpu.get_barrier_semaphore()
    for peer in peers:
        pl.semaphore_signal(barrier, inc=1, device_id=peer, device_id_type=MESH)

    own = shard(x, core, z)
    routes, gates = routes_ref[...], gates_ref[...]
    lane = lax.broadcasted_iota(jnp.int32, (R, 128), 1)
    rest = jnp.zeros((R, 128), F32)
    for k in range(routes.shape[1]):
        rest += jnp.where(routes[:, k : k + 1] == lane, gates[:, k : k + 1], F32(0))
    mine, tail = None, None
    for q in range(Q):
        place = selector(R * Q, R, -Q, q)
        term = jnp.dot(place, tok_ref[:, q * KC : (q + 1) * KC], preferred_element_type=F32)
        mine = term if mine is None else mine + term
        if q < 3:
            piece = rest.astype(BF16)
            rest = rest - piece.astype(F32)
            term = jnp.dot(place, piece, preferred_element_type=F32)
            tail = term if tail is None else tail + term
    buf[own, :, :KC] = mine.astype(BF16)
    buf[own, :, KC:] = tail.astype(BF16)
    pl.semaphore_wait(barrier, len(peers))

    def remote(src, dst, send, recv, to):
        return pltpu.make_async_remote_copy(
            src_ref=src, dst_ref=dst, send_sem=send, recv_sem=recv, device_id=to, device_id_type=MESH
        )

    def ag(s, send, to):
        return remote(buf.at[s], buf.at[s], send, ag_recv.at[s], to)

    sends = []

    def go(copy):
        copy.start()
        sends.append(copy)

    def peer_z(j):
        if NZ != 4:
            return (z + j) % NZ
        return (z, z + 1 - 2 * (z % 2), (z + 2) % 4, 3 - z)[j]

    def to_x(j):
        s = shard(x, core, peer_z(j))
        for k in range(1, NX):
            go(ag(s, agx_sem.at[j, k - 1], dev((x + k) % NX, core, z)))

    def to_core(i, j):
        s = shard((x + i) % NX, core, peer_z(j))
        go(ag(s, agc_sem.at[i, j], dev(x, other, z)))

    def arrived(s):
        ag(s, agz_sem.at[0], dev(x, other, z)).wait_recv()

    for k in range(1, NZ):
        go(ag(own, agz_sem.at[k - 1], dev(x, core, peer_z(k))))
    to_x(0)
    to_core(0, 0)
    for j in range(1, NZ):
        arrived(shard(x, core, peer_z(j)))
        to_x(j)
        to_core(0, j)
    for j in range(NZ):
        for i in range(1, NX):
            arrived(shard((x + i) % NX, core, peer_z(j)))
            to_core(i, j)
    for i in range(NX):
        for j in range(NZ):
            arrived(shard((x + i) % NX, other, (z + j) % NZ))

    S = NX * NZ * NCORE
    G = min(S, 16)
    for g in range(S // G):
        rows = pl.ds(g * G * R, G * R)
        block = buf[g * G : (g + 1) * G].reshape(G * R * Q, buf.shape[2])
        weight = None
        for q in range(Q):
            pick = selector(G * R, G * R * Q, Q, q)
            got = jnp.dot(pick, block, preferred_element_type=F32)
            xs[q, rows, :] = got[:, :KC].astype(BF16)
            tail = got[:, KC:]
            weight = tail if weight is None else weight + tail
        wts[rows, :] = weight

    def gu_step(i, carry):
        e, q = i // Q, i % Q
        slot = i % NG
        gu_copy(i, 0).wait()
        gu_copy(i, 1).wait()
        rows = xs[q]
        g = jnp.dot(rows, gu[slot, 0], preferred_element_type=F32)
        u = jnp.dot(rows, gu[slot, 1], preferred_element_type=F32)

        @pl.when(q == 0)
        def _():
            acc_g[...] = g
            acc_u[...] = u

        @pl.when(q > 0)
        def _():
            acc_g[...] += g
            acc_u[...] += u

        @pl.when(q == Q - 1)
        def _():
            lane = lax.broadcasted_iota(jnp.int32, wts.shape, 1)
            scale = jnp.sum(jnp.where(lane == ex * EL + e, wts[...], F32(0)), axis=1, keepdims=True)
            gate = acc_g[...]
            hid[e] = (gate / (1 + jnp.exp(-gate)) * acc_u[...] * scale).astype(BF16)

        nxt = i + NG

        @pl.when(nxt < NGU)
        def _():
            gu_copy(nxt, 0).start()
            gu_copy(nxt, 1).start()

        return carry

    lax.fori_loop(0, NGU, gu_step, 0)

    def send1(c):
        return remote(s1.at[c], r1.at[c], s1_sem.at[c], r1_sem.at[c], dev(x, other, z))

    def send2(c, k):
        return remote(
            s2.at[c, k - 1], r2.at[c, k - 1], s2_sem.at[c, k - 1], r2_sem.at[c, k - 1],
            dev((x + k) % NX, core, z),
        )

    def send3(c, k):
        to = (z + k) % NZ
        return remote(
            s3.at[c, to], r3.at[c, k - 1], s3_sem.at[c, k - 1], r3_sem.at[c, k - 1], dev(x, core, to)
        )

    def down_step(t, carry):
        @pl.when(t < NC)
        def _():
            dn_copy(t).wait()
            slot = t % ND
            total = jnp.dot(hid[0], dn[slot, 0], preferred_element_type=F32)
            for e in range(1, EL):
                total += jnp.dot(hid[e], dn[slot, e], preferred_element_type=F32)
            part[t % (LAG + 1)] = total.reshape(part.shape[1:])
            s1[t] = part[t % (LAG + 1), other].astype(BF16)
            send1(t).start()

            @pl.when(t + ND < NC)
            def _():
                dn_copy(t + ND).start()

        @pl.when((t >= LAG) & (t < NC + LAG))
        def _():
            c = t - LAG
            send1(c).wait_recv()
            y = part[c % (LAG + 1), core] + r1[c].astype(F32)
            part2[c % (LAG + 1)] = y.reshape(part2.shape[1:])
            for k in range(1, NX):
                s2[c, k - 1] = part2[c % (LAG + 1), (x + k) % NX].astype(BF16)
                send2(c, k).start()

        @pl.when((t >= 2 * LAG) & (t < NC + 2 * LAG))
        def _():
            c = t - 2 * LAG
            y = part2[c % (LAG + 1), x]
            for k in range(1, NX):
                send2(c, k).wait_recv()
                y += r2[c, k - 1].astype(F32)
            y = y.astype(BF16)
            w = C // Q
            packed = None
            for q in range(Q):
                pick = selector(NZ * R * Q, NZ * R, -Q, q)
                term = jnp.dot(pick, y[:, q * w : (q + 1) * w], preferred_element_type=F32)
                packed = term if packed is None else packed + term
            s3[c] = packed.astype(BF16).reshape(NZ, R * Q, w)
            for k in range(1, NZ):
                send3(c, k).start()

        @pl.when(t >= 3 * LAG)
        def _():
            c = t - 3 * LAG
            y = s3[c, z].astype(F32)
            for k in range(1, NZ):
                send3(c, k).wait_recv()
                y += r3[c, k - 1].astype(F32)
            y = y.astype(BF16)
            w = C // Q
            for q in range(Q):
                pick = selector(R, R * Q, Q, q)
                piece = jnp.dot(pick, y, preferred_element_type=F32).astype(BF16)
                out_ref[:, pl.ds(pl.multiple_of(c * C + q * w, 128), w)] = piece

        return carry

    lax.fori_loop(0, NC + 3 * LAG, down_step, 0)

    for copy in sends:
        copy.wait_send()

    def finish(c, carry):
        send1(c).wait_send()
        for k in range(1, NX):
            send2(c, k).wait_send()
        for k in range(1, NZ):
            send3(c, k).wait_send()
        return carry

    lax.fori_loop(0, NC, finish, 0)


def shards(tokens, routes, gates, w_gate, w_up, w_down):
    n_expert, n_split = lax.axis_size("expert"), lax.axis_size("split")
    R, D = tokens.shape
    EL, _, FF = w_gate.shape
    Q = 16 // R
    NCORE = 2
    NX, NZ = n_expert // NCORE, n_split
    KC = D // Q
    C = 512
    NC = D // C
    NG, ND = min(7, EL * Q), min(10, NC)
    M = NX * NZ * NCORE * R
    S = NX * NZ * NCORE
    cfg = dict(NX=NX, NZ=NZ, NCORE=NCORE, R=R, Q=Q, EL=EL, NG=NG, ND=ND, NC=NC, C=C, FF=FF)

    any_space = pl.BlockSpec(memory_space=pl.ANY)
    vmem = pl.BlockSpec(memory_space=pltpu.VMEM)
    dma = pltpu.SemaphoreType.DMA
    out = pl.pallas_call(
        functools.partial(kernel, cfg),
        out_shape=jax.ShapeDtypeStruct((R, D), BF16),
        in_specs=[vmem, vmem, vmem, any_space, any_space, any_space],
        out_specs=vmem,
        scratch_shapes=[
            pltpu.VMEM((S, R * Q, KC + 128), BF16),
            pltpu.VMEM((Q, M, KC), BF16),
            pltpu.VMEM((M, 128), F32),
            pltpu.VMEM((NG, 2, KC, FF), BF16),
            pltpu.VMEM((ND, EL, FF, C), BF16),
            pltpu.VMEM((M, FF), F32),
            pltpu.VMEM((M, FF), F32),
            pltpu.VMEM((EL, M, FF), BF16),
            pltpu.VMEM((LAG + 1, NCORE, M // NCORE, C), F32),
            pltpu.VMEM((LAG + 1, NX, NZ * R, C), F32),
            pltpu.VMEM((NC, M // NCORE, C), BF16),
            pltpu.VMEM((NC, M // NCORE, C), BF16),
            pltpu.VMEM((NC, NX - 1, NZ * R, C), BF16),
            pltpu.VMEM((NC, NX - 1, NZ * R, C), BF16),
            pltpu.VMEM((NC, NZ, R * Q, C // Q), BF16),
            pltpu.VMEM((NC, NZ - 1, R * Q, C // Q), BF16),
            dma((NG, 2)), dma((ND,)), dma((NZ - 1,)), dma((NZ, NX - 1)), dma((NX, NZ)), dma((S,)),
            dma((NC,)), dma((NC,)), dma((NC, NX - 1)), dma((NC, NX - 1)), dma((NC, NZ - 1)), dma((NC, NZ - 1)),
        ],
        compiler_params=pltpu.CompilerParams(
            collective_id=0, has_side_effects=True, vmem_limit_bytes=60 * 1024 * 1024
        ),
        cost_estimate=pl.CostEstimate(
            flops=6 * M * EL * D * FF, bytes_accessed=6 * EL * D * FF, transcendentals=M * EL * FF
        ),
        name="expert_layer",
    )(tokens, routes, gates, w_gate, w_up, w_down)
    return out


def solution(mesh):
    in_specs = (
        P(("parts", "expert", "split"), None),
        P(("parts", "expert", "split"), None),
        P(("parts", "expert", "split"), None),
        P("expert", None, "split"),
        P("expert", None, "split"),
        P("expert", "split", None),
    )
    out_specs = P(("parts", "expert", "split"), None)
    return jax.shard_map(shards, mesh=mesh, in_specs=in_specs, out_specs=out_specs, check_vma=False)
```
